32 devices in a mesh: tm: 4 (over x, core), coef: 8 (over z, y).
Axes of the slice: x: 2, y: 2, z: 4, core: 2. Of those that a mesh axis runs over, the one named last changes fastest.
Arguments:
- design: float32 [2048, 40960], P('tm', 'coef'), may hold values from -4 to 4
- whitening: float32 [2048, 256], P('tm'), may hold values from -1 to 3, as said below
- solution: float32 [40960, 64], P('coef'), may hold values from -6 to 6
- direction: float32 [40960, 64], P('coef'), may hold values from -6 to 6
- gradient_prev: float32 [40960, 64], P('coef'), may hold values from -25 to 25
- residual: float32 [2048, 64], P('tm'), may hold values from -6 to 6
Outputs:
- new_solution: float32 [40960, 64], P('coef')
- new_residual: float32 [2048, 64], P('tm')
- new_direction: float32 [40960, 64], P('coef')
The draws below stay inside these ranges and needn't reach their ends.
Inputs may be any that keep to these rules, and one draw needn't show every extreme that they name: `whitening`: the first tap of every row is positive.
All inputs are finite; a program needn't handle non-finite values.
Results may differ from the reference program's by a relative error of at most 0.00008.
Values sent between devices are 32-bit elements; how exact they have to be, the bound alone decides.
A program may use at most 64 MiB of HBM per device.

```python
import math
import jax
import jax.numpy as jnp
from jax import lax

NC = 40960
R = 64
BW = 256
ROWS = 2048


def column_scales(key_scale, count):
    rising = 3.0 ** (jnp.arange(count, dtype=jnp.float32) / count)
    return jnp.exp(jax.random.uniform(key_scale, (count,), jnp.float32) * math.log(10.0)) * rising


def draw_whitening(key, part):
    key_scale = jax.random.fold_in(key, 11)
    key_lead = jax.random.fold_in(key, 12)
    key_tail = jax.random.fold_in(key, 13)
    row_scale = column_scales(key_scale, ROWS)[:, None] * 0.033
    leading = jax.random.uniform(key_lead, (ROWS, 1), jnp.float32, 1.0, 2.0)
    trailing = jnp.clip(jax.random.normal(key_tail, (ROWS, BW - 1), jnp.float32), -4.0, 4.0) * 0.05
    return jnp.concatenate([leading, trailing], axis=1) * row_scale


def draw_design(key, part):
    key_scale = jax.random.fold_in(key, 21)
    key_base = jax.random.fold_in(key, 22)
    scales = column_scales(key_scale, NC)[None, :] / (2.2 * math.sqrt(NC))
    base_values = jnp.clip(jax.random.normal(key_base, (ROWS, NC), jnp.float32), -4.0, 4.0)
    return base_values * scales


def draw_gradient_prev(key, part):
    key_scale = jax.random.fold_in(key, 31)
    key_base = jax.random.fold_in(key, 32)
    scales = column_scales(key_scale, NC)[:, None] * 0.145
    base_values = jnp.clip(jax.random.normal(key_base, (NC, R), jnp.float32), -4.0, 4.0)
    return base_values * scales


def block_levels(rng, extent, pieces, low, largest):
    def one(axis_at, blocks):
        heights = jax.random.uniform(jax.random.fold_in(jax.random.fold_in(rng, 6), axis_at), (blocks,), jnp.float32, low / len(pieces), largest / len(pieces))
        return jnp.repeat(jnp.exp(heights), extent[axis_at] // blocks).reshape((-1,) + (1,) * (len(extent) - axis_at - 1))

    gain = one(*pieces[0])
    for cut in pieces[1:]:
        gain = gain * one(*cut)
    return gain


def gaussian(own_key, shape, deviation, most, shards=(), kind=jnp.bfloat16):
    entries = deviation * jax.random.normal(own_key, shape, jnp.float32)
    if shards:
        entries = entries * block_levels(own_key, shape, shards, -0.22, 0.18)
    return jnp.clip(entries, -most, most).astype(kind)


def setup_inputs(seed: int = 0) -> dict:
    seeds = jax.random.split(jax.random.key(seed), 7)
    return {
        "design": draw_design(jax.random.fold_in(seeds[6], 71), 0),
        "whitening": draw_whitening(jax.random.fold_in(seeds[6], 71), 0),
        "solution": gaussian(seeds[2], (NC, R), 1.0, 6.0, ((0, 8),), jnp.float32),
        "direction": gaussian(seeds[3], (NC, R), 1.0, 6.0, ((0, 8),), jnp.float32),
        "gradient_prev": draw_gradient_prev(jax.random.fold_in(seeds[6], 71), 0),
        "residual": gaussian(seeds[5], (ROWS, R), 1.0, 6.0, ((0, 4),), jnp.float32),
    }


def whiten(values, taps):
    rows_all = values.shape[0]
    lag = taps.shape[1]
    padded = jnp.concatenate([jnp.zeros((lag - 1, values.shape[1]), values.dtype), values], axis=0)

    def add_tap(offset, total):
        start = (lag - 1 - offset).astype(jnp.int32)
        shifted = lax.dynamic_slice_in_dim(padded, start, rows_all, 0)
        column = lax.dynamic_slice_in_dim(taps, offset.astype(jnp.int32), 1, 1)
        return total + column * shifted

    return lax.fori_loop(jnp.int32(0), jnp.int32(lag), add_tap, jnp.zeros_like(values))


def unwhiten(values, taps):
    rows_all = values.shape[0]
    lag = taps.shape[1]
    tail_zeros = jnp.zeros((lag - 1, values.shape[1]), values.dtype)

    def add_tap(offset, total):
        column = lax.dynamic_slice_in_dim(taps, offset.astype(jnp.int32), 1, 1)
        padded = jnp.concatenate([column * values, tail_zeros], axis=0)
        return total + lax.dynamic_slice_in_dim(padded, offset.astype(jnp.int32), rows_all, 0)

    return lax.fori_loop(jnp.int32(0), jnp.int32(lag), add_tap, jnp.zeros_like(values))


def reference(design, whitening, solution, direction, gradient_prev, residual):
    old_norm = jnp.sum(gradient_prev * gradient_prev, axis=0)
    plain = jnp.dot(design, direction, precision=lax.Precision.HIGHEST, preferred_element_type=jnp.float32)
    predicted = whiten(plain, whitening)
    energy = jnp.sum(predicted * predicted, axis=0)
    step_size = old_norm / energy
    new_solution = solution + step_size * direction
    new_residual = residual - step_size * predicted
    whitened = unwhiten(new_residual, whitening)
    gradient = lax.dot_general(design, whitened, (((0,), (0,)), ((), ())), precision=lax.Precision.HIGHEST, preferred_element_type=jnp.float32)
    new_norm = jnp.sum(gradient * gradient, axis=0)
    new_direction = gradient + (new_norm / old_norm) * direction
    return new_solution, new_residual, new_direction
```

```python
import functools

import jax
import jax.numpy as jnp
from jax import lax
from jax.experimental import pallas as pl
from jax.experimental.pallas import tpu as pltpu
from jax.sharding import PartitionSpec as P

F32 = jnp.float32
BF16 = jnp.bfloat16
LANES = 128


def chunk_width(columns):
    for width in (512, 384, 256, 128):
        if columns % (2 * width) == 0:
            return width
    return columns // 2


def split(x):
    hi = x.astype(BF16)
    return hi, (x - hi.astype(F32)).astype(BF16)


def dot_nt(a, b):
    return lax.dot_general(a, b, (((1,), (1,)), ((), ())), preferred_element_type=F32)


def dot_nn(a, b):
    return jnp.dot(a, b, preferred_element_type=F32)


def lane_fold(x):
    total = x[:, :LANES]
    for at in range(LANES, x.shape[1], LANES):
        total = total + x[:, at : at + LANES]
    return total


def total_over_lanes(x):
    return jnp.broadcast_to(jnp.sum(x, axis=1, keepdims=True), x.shape)


def widen(x, columns):
    return jnp.concatenate([x] * (columns // LANES), axis=1)


def kernel(
    ntm, ncoef,
    design, whitening, sol, direction, gprev, resid,
    nsol_out, nres_out, ndir_out,
    df, dhi, dlo, dv, gp, sv, rv, wv, acc, band_hi, band_lo,
    rs_send, rs_recv, halo_send, halo_recv, e_buf, carry_send, carry_recv,
    ag_buf, ag2_buf, white, nres, nsol, psend, precv, xbuf, gbuf, nd, n_buf,
    sem_d, sem_v, sem_in, sem_out, sem_nd,
    rs_s, rs_r, halo_s, halo_r, e_s, e_r, carry_s, carry_r,
    ag_s, ag_r, ag2_s, ag2_r, pair_s, pair_r, x_s, x_r, fin_s, fin_r, n_s, n_r,
):
    nch, count, width = df.shape
    half = nch // 2
    nchip = ntm // 2
    right_sides = dv.shape[1]
    rpc = right_sides // ncoef
    bw = whitening.shape[1]
    nblocks = count // bw
    tm = lax.axis_index("tm")
    coef = lax.axis_index("coef")
    core = lax.rem(tm, 2)
    chip = tm // 2
    partner = chip * 2 + (1 - core)
    MESH = pl.DeviceIdType.MESH

    def remote(src, dst, send, recv, to):
        copy = pltpu.make_async_remote_copy(
            src_ref=src, dst_ref=dst, send_sem=send, recv_sem=recv,
            device_id=to, device_id_type=MESH,
        )
        return copy

    wh_copy = pltpu.make_async_copy(whitening, wv, sem_in.at[0])
    wh_copy.start()

    def cols(i):
        return pl.ds(pl.multiple_of(i * width, width), width)

    def d_copy(i):
        return pltpu.make_async_copy(design.at[:, cols(i)], df.at[i], sem_d.at[i])

    def v_copy(i):
        return pltpu.make_async_copy(direction.at[:, cols(i)], dv.at[i], sem_v.at[i])

    for i in range(nch):
        v_copy(i).start()
        d_copy(i).start()
    gp_copy = pltpu.make_async_copy(gprev, gp, sem_in.at[1])
    gp_copy.start()
    res_copy = pltpu.make_async_copy(resid, rv, sem_in.at[2])
    res_copy.start()
    sol_copy = pltpu.make_async_copy(sol, sv, sem_in.at[3])
    sol_copy.start()

    barrier = pltpu.get_barrier_semaphore()
    greeted = 0
    for d in range(ncoef):
        other = lax.rem(coef + d, ncoef)
        if d:
            pl.semaphore_signal(barrier, inc=1, device_id=(tm, other), device_id_type=MESH)
            greeted += 1
            pl.semaphore_signal(barrier, inc=1, device_id=(partner, other), device_id_type=MESH)
            greeted += 1
    for d in range(1, ntm):
        pl.semaphore_signal(
            barrier, inc=1, device_id=(lax.rem(tm + d, ntm), coef), device_id_type=MESH
        )
        greeted += 1

    wh_copy.wait()
    mirror = (
        lax.broadcasted_iota(jnp.int32, (bw, bw), 0)
        + lax.broadcasted_iota(jnp.int32, (bw, bw), 1)
        == bw - 1
    ).astype(F32)
    for b in range(nblocks):
        taps = jnp.dot(
            wv[b * bw : (b + 1) * bw, :], mirror,
            precision=lax.Precision.HIGHEST, preferred_element_type=F32,
        )
        padded = jnp.concatenate([taps, jnp.zeros((bw, bw), F32)], axis=1)
        band = pltpu.roll(padded, 1, 1, stride=1, stride_axis=0)
        hi, lo = split(band)
        band_hi[b] = hi
        band_lo[b] = lo

    acc[...] = jnp.zeros_like(acc)

    def forward(i, carry):
        d_copy(i).wait()
        v_copy(i).wait()
        hi, lo = split(df[i])
        dhi[i] = hi
        dlo[i] = lo
        vhi = dv[i].astype(BF16).astype(F32)
        both = jnp.concatenate([vhi, dv[i] - vhi], axis=0).astype(BF16)
        acc[...] += dot_nt(hi, both) + dot_nt(lo, both)
        return carry

    lax.fori_loop(0, nch, forward, 0)
    turned = acc[...].T
    partial = turned[:right_sides] + turned[right_sides:]
    gp_copy.wait()
    old_lanes = jnp.zeros((right_sides, LANES), F32)
    for i in range(nch):
        g = gp[:, i * width : (i + 1) * width]
        old_lanes = old_lanes + lane_fold(g * g)
    for j in range(ncoef):
        rs_send[j, :, :count] = partial[j * rpc : (j + 1) * rpc]
        rs_send[j, :, count:] = old_lanes[j * rpc : (j + 1) * rpc]

    pl.semaphore_wait(barrier, greeted)
    sends = []

    def start(copy):
        copy.start()
        sends.append(copy)

    peers = [lax.rem(coef + d, ncoef) for d in range(1, ncoef)]
    for j in peers:
        start(remote(rs_send.at[j], rs_recv.at[coef], rs_s.at[j], rs_r.at[coef], (tm, j)))
    rs_recv[coef] = rs_send[coef]

    res_copy.wait()
    for j in range(ncoef):
        ag2_buf[j, :, :count] = rv[j * rpc : (j + 1) * rpc, :]
    my_res = ag2_buf[coef][:, :count]

    def back(values):
        hi, lo = split(values)
        pieces = []
        for b in range(nblocks):
            h = hi[:, b * bw : (b + 1) * bw]
            l = lo[:, b * bw : (b + 1) * bw]
            pieces.append(
                dot_nn(h, band_hi[b]) + dot_nn(l, band_hi[b]) + dot_nn(h, band_lo[b])
            )
        out = [pieces[0][:, :bw]]
        for b in range(nblocks):
            tail = pieces[b][:, bw:]
            out.append(tail + pieces[b + 1][:, :bw] if b + 1 < nblocks else tail)
        return out[0], jnp.concatenate(out[1:], axis=1)

    res_out, res_in = back(my_res)

    for j in peers:
        remote(rs_send.at[j], rs_recv.at[j], rs_s.at[j], rs_r.at[j], (tm, j)).wait_recv()
    mine = rs_recv[0]
    for j in range(1, ncoef):
        mine = mine + rs_recv[j]
    total = mine[:, :count]
    old_norm = total_over_lanes(mine[:, count:])
    halo_send[...] = total[:, count - bw :]
    after = lax.rem(tm + 1, ntm)
    before = lax.rem(tm + ntm - 1, ntm)
    halo = remote(halo_send, halo_recv, halo_s, halo_r, (after, coef))
    start(halo)

    def forth(window, b):
        hi, lo = split(window)
        return dot_nt(hi, band_hi[b]) + dot_nt(lo, band_hi[b]) + dot_nt(hi, band_lo[b])

    later = [forth(total[:, (b - 1) * bw : (b + 1) * bw], b) for b in range(1, nblocks)]
    halo.wait_recv()
    edge = jnp.where(tm == 0, jnp.zeros_like(halo_recv[...]), halo_recv[...])
    first = forth(jnp.concatenate([edge, total[:, :bw]], axis=1), 0)
    predicted = jnp.concatenate([first] + later, axis=1)
    e_buf[tm] = lane_fold(predicted * predicted)
    for d in range(1, ntm):
        other = lax.rem(tm + d, ntm)
        start(remote(e_buf.at[tm], e_buf.at[tm], e_s.at[other], e_r.at[tm], (other, coef)))
    pred_out, pred_in = back(predicted)
    carry_send[:, :bw] = res_out
    carry_send[:, bw:] = pred_out
    carry = remote(carry_send, carry_recv, carry_s, carry_r, (before, coef))
    start(carry)
    for d in range(1, ntm):
        other = lax.rem(tm + d, ntm)
        remote(e_buf.at[other], e_buf.at[other], e_s.at[other], e_r.at[other], (other, coef)).wait_recv()
    energy = e_buf[0]
    for t in range(1, ntm):
        energy = energy + e_buf[t]
    step = old_norm / total_over_lanes(energy)
    carry.wait_recv()
    last = tm == ntm - 1
    carried = jnp.where(last, jnp.zeros_like(carry_recv[...]), carry_recv[...])

    def with_carried(inner, extra):
        tail = inner[:, count - bw :] + extra
        if count == bw:
            return tail
        return jnp.concatenate([inner[:, : count - bw], tail], axis=1)

    step_wide = widen(step, count)
    ag_buf[coef] = with_carried(res_in, carried[:, :bw]) - step_wide * with_carried(
        pred_in, carried[:, bw:]
    )
    for j in peers:
        start(remote(ag_buf.at[coef], ag_buf.at[coef], ag_s.at[j], ag_r.at[coef], (tm, j)))
    ag2_buf[coef, :, :count] = my_res - step_wide * predicted
    ag2_buf[coef, :, count : count + LANES] = step
    ag2_buf[coef, :, count + LANES :] = old_norm
    for j in peers:
        remote(ag_buf.at[j], ag_buf.at[j], ag_s.at[j], ag_r.at[j], (tm, j)).wait_recv()
    for j in range(ncoef):
        white[j * rpc : (j + 1) * rpc, :] = ag_buf[j]
    whi = white[...].astype(BF16)
    whi32 = whi.astype(F32)
    wboth = jnp.concatenate([whi32, white[...] - whi32], axis=0).astype(BF16)

    def grad_chunk(i):
        a = dot_nn(wboth, dhi[i])
        return a[:right_sides] + a[right_sides:] + dot_nn(whi, dlo[i])

    def to_chips(k):
        remote(psend.at[k], precv.at[k], pair_s.at[k], pair_r.at[k], (partner, coef)).wait_recv()
        xbuf[chip, k] = xbuf[chip, k] + precv[k]
        for q in range(1, nchip):
            other = lax.rem(chip + q, nchip)
            start(
                remote(
                    xbuf.at[chip, k], xbuf.at[chip, k], x_s.at[other, k], x_r.at[chip, k],
                    (other * 2 + core, coef),
                )
            )

    for k in range(half):
        psend[k] = grad_chunk((1 - core) * half + k)
        start(remote(psend.at[k], precv.at[k], pair_s.at[k], pair_r.at[k], (partner, coef)))
        xbuf[chip, k] = grad_chunk(core * half + k)
        to_chips(k)
        if k == 0:
            for j in peers:
                start(
                    remote(ag2_buf.at[coef], ag2_buf.at[coef], ag2_s.at[j], ag2_r.at[coef], (tm, j))
                )

    for j in peers:
        remote(ag2_buf.at[j], ag2_buf.at[j], ag2_s.at[j], ag2_r.at[j], (tm, j)).wait_recv()
    tails = []
    for j in range(ncoef):
        nres[j * rpc : (j + 1) * rpc, :] = ag2_buf[j][:, :count]
        tails.append(ag2_buf[j][:, count:])
    tail = jnp.concatenate(tails, axis=0)
    step_all = widen(tail[:, :LANES], width)
    old_all = tail[:, LANES:]
    nres_copy = pltpu.make_async_copy(nres, nres_out, sem_out.at[0])
    nres_copy.start()
    sol_copy.wait()
    for i in range(nch):
        at = slice(i * width, (i + 1) * width)
        nsol[:, at] = sv[:, at] + step_all * dv[i]
    nsol_copy = pltpu.make_async_copy(nsol, nsol_out, sem_out.at[1])
    nsol_copy.start()

    squares = jnp.zeros((right_sides, LANES), F32)
    for k in range(half):
        for q in range(1, nchip):
            other = lax.rem(chip + q, nchip)
            remote(
                xbuf.at[other, k], xbuf.at[other, k], x_s.at[other, k], x_r.at[other, k],
                (other * 2 + core, coef),
            ).wait_recv()
        g = xbuf[0, k]
        for t in range(1, nchip):
            g = g + xbuf[t, k]
        at = core * half + k
        gbuf[at] = g
        start(remote(gbuf.at[at], gbuf.at[at], fin_s.at[k], fin_r.at[k], (partner, coef)))
        squares = squares + lane_fold(g * g)

    slot = coef * 2 + core
    row = jnp.sum(squares.T, axis=0, keepdims=True)
    n_buf[slot] = jnp.concatenate([row, jnp.zeros((1, LANES - right_sides), F32)], axis=1)
    others = [(tm, j, j * 2 + core) for j in peers]
    others += [(partner, j, j * 2 + (1 - core)) for j in [coef] + peers]
    for t, j, s in others:
        start(remote(n_buf.at[slot], n_buf.at[slot], n_s.at[s], n_r.at[slot], (t, j)))
    for k in range(half):
        at = (1 - core) * half + k
        remote(gbuf.at[at], gbuf.at[at], fin_s.at[k], fin_r.at[k], (partner, coef)).wait_recv()
    for t, j, s in others:
        remote(n_buf.at[s], n_buf.at[s], n_s.at[s], n_r.at[s], (t, j)).wait_recv()
    row = n_buf[0]
    for s in range(1, 2 * ncoef):
        row = row + n_buf[s]
    new_all = jnp.broadcast_to(row, (LANES, LANES)).T[:right_sides]
    ratio = widen(new_all / old_all, width)
    outs = []
    for i in range(nch):
        nd[i] = gbuf[i] + ratio * dv[i]
        copy = pltpu.make_async_copy(
            nd.at[i], ndir_out.at[:, i * width : (i + 1) * width], sem_nd.at[i]
        )
        copy.start()
        outs.append(copy)
    for copy in sends:
        copy.wait_send()
    nres_copy.wait()
    nsol_copy.wait()
    for copy in outs:
        copy.wait()


def per_device(ntm, ncoef, design, whitening, solution, direction, gradient_prev, residual):
    count, columns = design.shape
    bw = whitening.shape[1]
    rs = direction.shape[1]
    rpc = rs // ncoef
    width = chunk_width(columns)
    nch = columns // width
    half = nch // 2
    nchip = ntm // 2
    nblocks = count // bw
    V = pltpu.VMEM
    D = pltpu.SemaphoreType.DMA
    any_spec = pl.BlockSpec(memory_space=pl.ANY)
    scratch = [
        V((nch, count, width), F32),
        V((nch, count, width), BF16),
        V((nch, count, width), BF16),
        V((nch, rs, width), F32),
        V((rs, columns), F32),
        V((rs, columns), F32),
        V((rs, count), F32),
        V((count, bw), F32),
        V((count, 2 * rs), F32),
        V((nblocks, bw, 2 * bw), BF16),
        V((nblocks, bw, 2 * bw), BF16),
        V((ncoef, rpc, count + LANES), F32),
        V((ncoef, rpc, count + LANES), F32),
        V((rpc, bw), F32),
        V((rpc, bw), F32),
        V((ntm, rpc, LANES), F32),
        V((rpc, 2 * bw), F32),
        V((rpc, 2 * bw), F32),
        V((ncoef, rpc, count), F32),
        V((ncoef, rpc, count + 2 * LANES), F32),
        V((rs, count), F32),
        V((rs, count), F32),
        V((rs, columns), F32),
        V((half, rs, width), F32),
        V((half, rs, width), F32),
        V((nchip, half, rs, width), F32),
        V((nch, rs, width), F32),
        V((nch, rs, width), F32),
        V((2 * ncoef, 1, LANES), F32),
        D((nch,)), D((nch,)), D((4,)), D((2,)), D((nch,)),
        D((ncoef,)), D((ncoef,)), D, D, D((ntm,)), D((ntm,)), D, D,
        D((ncoef,)), D((ncoef,)), D((ncoef,)), D((ncoef,)),
        D((half,)), D((half,)), D((nchip, half)), D((nchip, half)),
        D((half,)), D((half,)), D((2 * ncoef,)), D((2 * ncoef,)),
    ]
    outs = pl.pallas_call(
        functools.partial(kernel, ntm, ncoef),
        out_shape=(
            jax.ShapeDtypeStruct((rs, columns), F32),
            jax.ShapeDtypeStruct((rs, count), F32),
            jax.ShapeDtypeStruct((rs, columns), F32),
        ),
        in_specs=[any_spec] * 6,
        out_specs=(any_spec,) * 3,
        scratch_shapes=scratch,
        compiler_params=pltpu.CompilerParams(
            collective_id=0, has_side_effects=True, vmem_limit_bytes=56 * 2**20
        ),
        cost_estimate=pl.CostEstimate(
            flops=12 * count * columns * rs,
            bytes_accessed=4 * (count * columns + 5 * rs * columns),
            transcendentals=0,
        ),
    )(design, whitening, solution.T, direction.T, gradient_prev.T, residual.T)
    return tuple(o.T for o in outs)


def solution(mesh):
    ntm, ncoef = mesh.shape["tm"], mesh.shape["coef"]
    return jax.shard_map(
        functools.partial(per_device, ntm, ncoef),
        mesh=mesh,
        in_specs=(
            P("tm", "coef"),
            P("tm", None),
            P("coef", None),
            P("coef", None),
            P("coef", None),
            P("tm", None),
        ),
        out_specs=(P("coef", None), P("tm", None), P("coef", None)),
        check_vma=False,
    )
```

```python
import functools

import jax
import jax.numpy as jnp
from jax import lax
from jax.experimental import pallas as pl
from jax.experimental.pallas import tpu as pltpu
from jax.sharding import PartitionSpec as P

F32 = jnp.float32
BF16 = jnp.bfloat16
LANES = 128


def chunk_width(columns):
    for width in (512, 384, 256, 128):
        if columns % (2 * width) == 0:
            return width
    return columns // 2


def split(x):
    hi = x.astype(BF16)
    return hi, (x - hi.astype(F32)).astype(BF16)


def dot_nt(a, b):
    return lax.dot_general(a, b, (((1,), (1,)), ((), ())), preferred_element_type=F32)


def dot_nn(a, b):
    return jnp.dot(a, b, preferred_element_type=F32)


def lane_fold(x):
    total = x[:, :LANES]
    for at in range(LANES, x.shape[1], LANES):
        total = total + x[:, at : at + LANES]
    return total


def total_over_lanes(x):
    return jnp.broadcast_to(jnp.sum(x, axis=1, keepdims=True), x.shape)


def widen(x, columns):
    return jnp.concatenate([x] * (columns // LANES), axis=1)


def kernel(
    ntm, ncoef,
    design, whitening, direction, gprev, resid,
    nres, grad, scale,
    df, dhi, dlo, dv, gp, rv, wv, acc, band_hi, band_lo,
    rs_send, rs_recv, halo_send, halo_recv, e_buf, carry_send, carry_recv,
    ag_buf, ag2_buf, white, psend, precv, xbuf, gbuf, n_buf,
    sem_d, sem_v, sem_in,
    rs_s, rs_r, halo_s, halo_r, e_s, e_r, carry_s, carry_r,
    ag_s, ag_r, ag2_s, ag2_r, pair_s, pair_r, x_s, x_r, fin_s, fin_r, n_s, n_r,
):
    nch, count, width = df.shape
    half = nch // 2
    nchip = ntm // 2
    right_sides = dv.shape[1]
    rpc = right_sides // ncoef
    bw = whitening.shape[1]
    nblocks = count // bw
    tm = lax.axis_index("tm")
    coef = lax.axis_index("coef")
    core = lax.rem(tm, 2)
    chip = tm // 2
    partner = chip * 2 + (1 - core)
    MESH = pl.DeviceIdType.MESH

    def remote(src, dst, send, recv, to):
        copy = pltpu.make_async_remote_copy(
            src_ref=src, dst_ref=dst, send_sem=send, recv_sem=recv,
            device_id=to, device_id_type=MESH,
        )
        return copy

    wh_copy = pltpu.make_async_copy(whitening, wv, sem_in.at[0])
    wh_copy.start()

    def cols(i):
        return pl.ds(pl.multiple_of(i * width, width), width)

    def d_copy(i):
        return pltpu.make_async_copy(design.at[:, cols(i)], df.at[i], sem_d.at[i])

    def v_copy(i):
        return pltpu.make_async_copy(direction.at[:, cols(i)], dv.at[i], sem_v.at[i])

    for i in range(nch):
        v_copy(i).start()
        d_copy(i).start()
    gp_copy = pltpu.make_async_copy(gprev, gp, sem_in.at[1])
    gp_copy.start()
    res_copy = pltpu.make_async_copy(resid, rv, sem_in.at[2])
    res_copy.start()

    barrier = pltpu.get_barrier_semaphore()
    greeted = 0
    for d in range(ncoef):
        other = lax.rem(coef + d, ncoef)
        if d:
            pl.semaphore_signal(barrier, inc=1, device_id=(tm, other), device_id_type=MESH)
            greeted += 1
            pl.semaphore_signal(barrier, inc=1, device_id=(partner, other), device_id_type=MESH)
            greeted += 1
    for d in range(1, ntm):
        pl.semaphore_signal(
            barrier, inc=1, device_id=(lax.rem(tm + d, ntm), coef), device_id_type=MESH
        )
        greeted += 1

    wh_copy.wait()
    mirror = (
        lax.broadcasted_iota(jnp.int32, (bw, bw), 0)
        + lax.broadcasted_iota(jnp.int32, (bw, bw), 1)
        == bw - 1
    ).astype(F32)
    for b in range(nblocks):
        taps = jnp.dot(
            wv[b * bw : (b + 1) * bw, :], mirror,
            precision=lax.Precision.HIGHEST, preferred_element_type=F32,
        )
        padded = jnp.concatenate([taps, jnp.zeros((bw, bw), F32)], axis=1)
        band = pltpu.roll(padded, 1, 1, stride=1, stride_axis=0)
        hi, lo = split(band)
        band_hi[b] = hi
        band_lo[b] = lo

    acc[...] = jnp.zeros_like(acc)

    def forward(i, carry):
        d_copy(i).wait()
        v_copy(i).wait()
        hi, lo = split(df[i])
        dhi[i] = hi
        dlo[i] = lo
        vhi = dv[i].astype(BF16).astype(F32)
        both = jnp.concatenate([vhi, dv[i] - vhi], axis=0).astype(BF16)
        acc[...] += dot_nt(hi, both) + dot_nt(lo, both)
        return carry

    lax.fori_loop(0, nch, forward, 0)
    turned = acc[...].T
    partial = turned[:right_sides] + turned[right_sides:]
    gp_copy.wait()
    old_lanes = jnp.zeros((right_sides, LANES), F32)
    for i in range(nch):
        g = gp[:, i * width : (i + 1) * width]
        old_lanes = old_lanes + lane_fold(g * g)
    for j in range(ncoef):
        rs_send[j, :, :count] = partial[j * rpc : (j + 1) * rpc]
        rs_send[j, :, count:] = old_lanes[j * rpc : (j + 1) * rpc]

    pl.semaphore_wait(barrier, greeted)
    sends = []

    def start(copy):
        copy.start()
        sends.append(copy)

    peers = [lax.rem(coef + d, ncoef) for d in range(1, ncoef)]
    for j in peers:
        start(remote(rs_send.at[j], rs_recv.at[coef], rs_s.at[j], rs_r.at[coef], (tm, j)))
    rs_recv[coef] = rs_send[coef]

    res_copy.wait()
    for j in range(ncoef):
        ag2_buf[j, :, :count] = rv[j * rpc : (j + 1) * rpc, :]
    my_res = ag2_buf[coef][:, :count]

    def back(values):
        hi, lo = split(values)
        pieces = []
        for b in range(nblocks):
            h = hi[:, b * bw : (b + 1) * bw]
            l = lo[:, b * bw : (b + 1) * bw]
            pieces.append(
                dot_nn(h, band_hi[b]) + dot_nn(l, band_hi[b]) + dot_nn(h, band_lo[b])
            )
        out = [pieces[0][:, :bw]]
        for b in range(nblocks):
            tail = pieces[b][:, bw:]
            out.append(tail + pieces[b + 1][:, :bw] if b + 1 < nblocks else tail)
        return out[0], jnp.concatenate(out[1:], axis=1)

    res_out, res_in = back(my_res)

    for j in peers:
        remote(rs_send.at[j], rs_recv.at[j], rs_s.at[j], rs_r.at[j], (tm, j)).wait_recv()
    mine = rs_recv[0]
    for j in range(1, ncoef):
        mine = mine + rs_recv[j]
    total = mine[:, :count]
    old_norm = total_over_lanes(mine[:, count:])
    halo_send[...] = total[:, count - bw :]
    after = lax.rem(tm + 1, ntm)
    before = lax.rem(tm + ntm - 1, ntm)
    halo = remote(halo_send, halo_recv, halo_s, halo_r, (after, coef))
    start(halo)

    def forth(window, b):
        hi, lo = split(window)
        return dot_nt(hi, band_hi[b]) + dot_nt(lo, band_hi[b]) + dot_nt(hi, band_lo[b])

    later = [forth(total[:, (b - 1) * bw : (b + 1) * bw], b) for b in range(1, nblocks)]
    halo.wait_recv()
    edge = jnp.where(tm == 0, jnp.zeros_like(halo_recv[...]), halo_recv[...])
    first = forth(jnp.concatenate([edge, total[:, :bw]], axis=1), 0)
    predicted = jnp.concatenate([first] + later, axis=1)
    e_buf[tm] = lane_fold(predicted * predicted)
    for d in range(1, ntm):
        other = lax.rem(tm + d, ntm)
        start(remote(e_buf.at[tm], e_buf.at[tm], e_s.at[other], e_r.at[tm], (other, coef)))
    pred_out, pred_in = back(predicted)
    carry_send[:, :bw] = res_out
    carry_send[:, bw:] = pred_out
    carry = remote(carry_send, carry_recv, carry_s, carry_r, (before, coef))
    start(carry)
    for d in range(1, ntm):
        other = lax.rem(tm + d, ntm)
        remote(e_buf.at[other], e_buf.at[other], e_s.at[other], e_r.at[other], (other, coef)).wait_recv()
    energy = e_buf[0]
    for t in range(1, ntm):
        energy = energy + e_buf[t]
    step = old_norm / total_over_lanes(energy)
    carry.wait_recv()
    last = tm == ntm - 1
    carried = jnp.where(last, jnp.zeros_like(carry_recv[...]), carry_recv[...])

    def with_carried(inner, extra):
        tail = inner[:, count - bw :] + extra
        if count == bw:
            return tail
        return jnp.concatenate([inner[:, : count - bw], tail], axis=1)

    step_wide = widen(step, count)
    ag_buf[coef] = with_carried(res_in, carried[:, :bw]) - step_wide * with_carried(
        pred_in, carried[:, bw:]
    )
    for j in peers:
        start(remote(ag_buf.at[coef], ag_buf.at[coef], ag_s.at[j], ag_r.at[coef], (tm, j)))
    ag2_buf[coef, :, :count] = my_res - step_wide * predicted
    ag2_buf[coef, :, count : count + LANES] = step
    ag2_buf[coef, :, count + LANES :] = old_norm
    for j in peers:
        remote(ag_buf.at[j], ag_buf.at[j], ag_s.at[j], ag_r.at[j], (tm, j)).wait_recv()
    for j in range(ncoef):
        white[j * rpc : (j + 1) * rpc, :] = ag_buf[j]
    whi = white[...].astype(BF16)
    whi32 = whi.astype(F32)
    wboth = jnp.concatenate([whi32, white[...] - whi32], axis=0).astype(BF16)

    def grad_chunk(i):
        a = dot_nn(wboth, dhi[i])
        return a[:right_sides] + a[right_sides:] + dot_nn(whi, dlo[i])

    def to_chips(k):
        remote(psend.at[k], precv.at[k], pair_s.at[k], pair_r.at[k], (partner, coef)).wait_recv()
        xbuf[chip, k] = xbuf[chip, k] + precv[k]
        for q in range(1, nchip):
            other = lax.rem(chip + q, nchip)
            start(
                remote(
                    xbuf.at[chip, k], xbuf.at[chip, k], x_s.at[other, k], x_r.at[chip, k],
                    (other * 2 + core, coef),
                )
            )

    for k in range(half):
        psend[k] = grad_chunk((1 - core) * half + k)
        start(remote(psend.at[k], precv.at[k], pair_s.at[k], pair_r.at[k], (partner, coef)))
        xbuf[chip, k] = grad_chunk(core * half + k)
        to_chips(k)
        if k == 0:
            for j in peers:
                start(
                    remote(ag2_buf.at[coef], ag2_buf.at[coef], ag2_s.at[j], ag2_r.at[coef], (tm, j))
                )

    for j in peers:
        remote(ag2_buf.at[j], ag2_buf.at[j], ag2_s.at[j], ag2_r.at[j], (tm, j)).wait_recv()
    tails = []
    for j in range(ncoef):
        nres[j * rpc : (j + 1) * rpc, :] = ag2_buf[j][:, :count]
        tails.append(ag2_buf[j][:, count:])
    tail = jnp.concatenate(tails, axis=0)
    scale[0] = tail[:, :LANES]
    old_all = tail[:, LANES:]

    squares = jnp.zeros((right_sides, LANES), F32)
    for k in range(half):
        for q in range(1, nchip):
            other = lax.rem(chip + q, nchip)
            remote(
                xbuf.at[other, k], xbuf.at[other, k], x_s.at[other, k], x_r.at[other, k],
                (other * 2 + core, coef),
            ).wait_recv()
        g = xbuf[0, k]
        for t in range(1, nchip):
            g = g + xbuf[t, k]
        at = core * half + k
        gbuf[at] = g
        start(remote(gbuf.at[at], gbuf.at[at], fin_s.at[k], fin_r.at[k], (partner, coef)))
        squares = squares + lane_fold(g * g)

    slot = coef * 2 + core
    row = jnp.sum(squares.T, axis=0, keepdims=True)
    n_buf[slot] = jnp.concatenate([row, jnp.zeros((1, LANES - right_sides), F32)], axis=1)
    others = [(tm, j, j * 2 + core) for j in peers]
    others += [(partner, j, j * 2 + (1 - core)) for j in [coef] + peers]
    for t, j, s in others:
        start(remote(n_buf.at[slot], n_buf.at[slot], n_s.at[s], n_r.at[slot], (t, j)))
    for k in range(half):
        at = (1 - core) * half + k
        remote(gbuf.at[at], gbuf.at[at], fin_s.at[k], fin_r.at[k], (partner, coef)).wait_recv()
    for t, j, s in others:
        remote(n_buf.at[s], n_buf.at[s], n_s.at[s], n_r.at[s], (t, j)).wait_recv()
    row = n_buf[0]
    for s in range(1, 2 * ncoef):
        row = row + n_buf[s]
    new_all = jnp.broadcast_to(row, (LANES, LANES)).T[:right_sides]
    scale[1] = new_all / old_all
    for i in range(nch):
        grad[:, i * width : (i + 1) * width] = gbuf[i]
    for copy in sends:
        copy.wait_send()


def per_device(ntm, ncoef, design, whitening, solution, direction, gradient_prev, residual):
    count, columns = design.shape
    bw = whitening.shape[1]
    rs = direction.shape[1]
    rpc = rs // ncoef
    width = chunk_width(columns)
    nch = columns // width
    half = nch // 2
    nchip = ntm // 2
    nblocks = count // bw
    V = pltpu.VMEM
    D = pltpu.SemaphoreType.DMA
    scratch = [
        V((nch, count, width), F32),
        V((nch, count, width), BF16),
        V((nch, count, width), BF16),
        V((nch, rs, width), F32),
        V((rs, columns), F32),
        V((rs, count), F32),
        V((count, bw), F32),
        V((count, 2 * rs), F32),
        V((nblocks, bw, 2 * bw), BF16),
        V((nblocks, bw, 2 * bw), BF16),
        V((ncoef, rpc, count + LANES), F32),
        V((ncoef, rpc, count + LANES), F32),
        V((rpc, bw), F32),
        V((rpc, bw), F32),
        V((ntm, rpc, LANES), F32),
        V((rpc, 2 * bw), F32),
        V((rpc, 2 * bw), F32),
        V((ncoef, rpc, count), F32),
        V((ncoef, rpc, count + 2 * LANES), F32),
        V((rs, count), F32),
        V((half, rs, width), F32),
        V((half, rs, width), F32),
        V((nchip, half, rs, width), F32),
        V((nch, rs, width), F32),
        V((2 * ncoef, 1, LANES), F32),
        D((nch,)), D((nch,)), D((3,)),
        D((ncoef,)), D((ncoef,)), D, D, D((ntm,)), D((ntm,)), D, D,
        D((ncoef,)), D((ncoef,)), D((ncoef,)), D((ncoef,)),
        D((half,)), D((half,)), D((nchip, half)), D((nchip, half)),
        D((half,)), D((half,)), D((2 * ncoef,)), D((2 * ncoef,)),
    ]
    new_residual, gradient, scale = pl.pallas_call(
        functools.partial(kernel, ntm, ncoef),
        out_shape=(
            jax.ShapeDtypeStruct((rs, count), F32),
            jax.ShapeDtypeStruct((rs, columns), F32),
            jax.ShapeDtypeStruct((2, rs, LANES), F32),
        ),
        in_specs=[pl.BlockSpec(memory_space=pltpu.HBM)] * 5,
        out_specs=(pl.BlockSpec(memory_space=pltpu.VMEM),) * 3,
        scratch_shapes=scratch,
        compiler_params=pltpu.CompilerParams(
            collective_id=0, has_side_effects=True, vmem_limit_bytes=54 * 2**20
        ),
        cost_estimate=pl.CostEstimate(
            flops=12 * count * columns * rs,
            bytes_accessed=4 * (count * columns + 5 * rs * columns),
            transcendentals=0,
        ),
    )(design, whitening, direction.T, gradient_prev.T, residual.T)
    step = scale[0, :, 0]
    ratio = scale[1, :, 0]
    new_solution = solution + step * direction
    new_direction = gradient.T + ratio * direction
    return new_solution, new_residual.T, new_direction


def solution(mesh):
    ntm, ncoef = mesh.shape["tm"], mesh.shape["coef"]
    return jax.shard_map(
        functools.partial(per_device, ntm, ncoef),
        mesh=mesh,
        in_specs=(
            P("tm", "coef"),
            P("tm", None),
            P("coef", None),
            P("coef", None),
            P("coef", None),
            P("tm", None),
        ),
        out_specs=(P("coef", None), P("tm", None), P("coef", None)),
        check_vma=False,
    )
```

```python
import functools

import jax
import jax.numpy as jnp
from jax import lax
from jax.experimental import pallas as pl
from jax.experimental.pallas import tpu as pltpu
from jax.sharding import PartitionSpec as P

F32 = jnp.float32
BF16 = jnp.bfloat16
LANES = 128


def chunk_width(columns):
    for width in (512, 384, 256, 128):
        if columns % (2 * width) == 0:
            return width
    return columns // 2


def split(x):
    hi = x.astype(BF16)
    return hi, (x - hi.astype(F32)).astype(BF16)


def dot_nt(a, b):
    return lax.dot_general(a, b, (((1,), (1,)), ((), ())), preferred_element_type=F32)


def dot_nn(a, b):
    return jnp.dot(a, b, preferred_element_type=F32)


def lane_fold(x):
    total = x[:, :LANES]
    for at in range(LANES, x.shape[1], LANES):
        total = total + x[:, at : at + LANES]
    return total


def total_over_lanes(x):
    return jnp.broadcast_to(jnp.sum(x, axis=1, keepdims=True), x.shape)


def widen(x, columns):
    return jnp.concatenate([x] * (columns // LANES), axis=1)


def kernel(
    ntm, ncoef,
    design, whitening, sol, direction, gprev, resid,
    nsol, nres, ndir,
    df, dhi, dlo, dv, gp, sv, rv, wv, acc, band_hi, band_lo,
    rs_send, rs_recv, halo_send, halo_recv, e_buf, carry_send, carry_recv,
    ag_buf, ag2_buf, white, psend, precv, xbuf, gbuf, n_buf,
    sem_d, sem_v, sem_in,
    rs_s, rs_r, halo_s, halo_r, e_s, e_r, carry_s, carry_r,
    ag_s, ag_r, ag2_s, ag2_r, pair_s, pair_r, x_s, x_r, fin_s, fin_r, n_s, n_r,
):
    nch, count, width = df.shape
    half = nch // 2
    nchip = ntm // 2
    right_sides = dv.shape[1]
    rpc = right_sides // ncoef
    bw = whitening.shape[1]
    nblocks = count // bw
    tm = lax.axis_index("tm")
    coef = lax.axis_index("coef")
    core = lax.rem(tm, 2)
    chip = tm // 2
    partner = chip * 2 + (1 - core)
    MESH = pl.DeviceIdType.MESH

    def remote(src, dst, send, recv, to):
        copy = pltpu.make_async_remote_copy(
            src_ref=src, dst_ref=dst, send_sem=send, recv_sem=recv,
            device_id=to, device_id_type=MESH,
        )
        return copy

    wh_copy = pltpu.make_async_copy(whitening, wv, sem_in.at[0])
    wh_copy.start()

    def cols(i):
        return pl.ds(pl.multiple_of(i * width, width), width)

    def d_copy(i):
        return pltpu.make_async_copy(design.at[:, cols(i)], df.at[i], sem_d.at[i])

    def v_copy(i):
        return pltpu.make_async_copy(direction.at[:, cols(i)], dv.at[i], sem_v.at[i])

    for i in range(nch):
        v_copy(i).start()
        d_copy(i).start()
    gp_copy = pltpu.make_async_copy(gprev, gp, sem_in.at[1])
    gp_copy.start()
    res_copy = pltpu.make_async_copy(resid, rv, sem_in.at[2])
    res_copy.start()
    sol_copy = pltpu.make_async_copy(sol, sv, sem_in.at[3])
    sol_copy.start()

    barrier = pltpu.get_barrier_semaphore()
    greeted = 0
    for d in range(ncoef):
        other = lax.rem(coef + d, ncoef)
        if d:
            pl.semaphore_signal(barrier, inc=1, device_id=(tm, other), device_id_type=MESH)
            greeted += 1
            pl.semaphore_signal(barrier, inc=1, device_id=(partner, other), device_id_type=MESH)
            greeted += 1
    for d in range(1, ntm):
        pl.semaphore_signal(
            barrier, inc=1, device_id=(lax.rem(tm + d, ntm), coef), device_id_type=MESH
        )
        greeted += 1

    wh_copy.wait()
    mirror = (
        lax.broadcasted_iota(jnp.int32, (bw, bw), 0)
        + lax.broadcasted_iota(jnp.int32, (bw, bw), 1)
        == bw - 1
    ).astype(F32)
    for b in range(nblocks):
        taps = jnp.dot(
            wv[b * bw : (b + 1) * bw, :], mirror,
            precision=lax.Precision.HIGHEST, preferred_element_type=F32,
        )
        padded = jnp.concatenate([taps, jnp.zeros((bw, bw), F32)], axis=1)
        band = pltpu.roll(padded, 1, 1, stride=1, stride_axis=0)
        hi, lo = split(band)
        band_hi[b] = hi
        band_lo[b] = lo

    acc[...] = jnp.zeros_like(acc)

    def forward(i, carry):
        d_copy(i).wait()
        v_copy(i).wait()
        hi, lo = split(df[i])
        dhi[i] = hi
        dlo[i] = lo
        vhi = dv[i].astype(BF16).astype(F32)
        both = jnp.concatenate([vhi, dv[i] - vhi], axis=0).astype(BF16)
        acc[...] += dot_nt(hi, both) + dot_nt(lo, both)
        return carry

    lax.fori_loop(0, nch, forward, 0)
    turned = acc[...].T
    partial = turned[:right_sides] + turned[right_sides:]
    gp_copy.wait()
    old_lanes = jnp.zeros((right_sides, LANES), F32)
    for i in range(nch):
        g = gp[:, i * width : (i + 1) * width]
        old_lanes = old_lanes + lane_fold(g * g)
    for j in range(ncoef):
        rs_send[j, :, :count] = partial[j * rpc : (j + 1) * rpc]
        rs_send[j, :, count:] = old_lanes[j * rpc : (j + 1) * rpc]

    pl.semaphore_wait(barrier, greeted)
    sends = []

    def start(copy):
        copy.start()
        sends.append(copy)

    peers = [lax.rem(coef + d, ncoef) for d in range(1, ncoef)]
    for j in peers:
        start(remote(rs_send.at[j], rs_recv.at[coef], rs_s.at[j], rs_r.at[coef], (tm, j)))
    rs_recv[coef] = rs_send[coef]

    res_copy.wait()
    for j in range(ncoef):
        ag2_buf[j, :, :count] = rv[j * rpc : (j + 1) * rpc, :]
    my_res = ag2_buf[coef][:, :count]

    def back(values):
        hi, lo = split(values)
        pieces = []
        for b in range(nblocks):
            h = hi[:, b * bw : (b + 1) * bw]
            l = lo[:, b * bw : (b + 1) * bw]
            pieces.append(
                dot_nn(h, band_hi[b]) + dot_nn(l, band_hi[b]) + dot_nn(h, band_lo[b])
            )
        out = [pieces[0][:, :bw]]
        for b in range(nblocks):
            tail = pieces[b][:, bw:]
            out.append(tail + pieces[b + 1][:, :bw] if b + 1 < nblocks else tail)
        return out[0], jnp.concatenate(out[1:], axis=1)

    res_out, res_in = back(my_res)

    for j in peers:
        remote(rs_send.at[j], rs_recv.at[j], rs_s.at[j], rs_r.at[j], (tm, j)).wait_recv()
    mine = rs_recv[0]
    for j in range(1, ncoef):
        mine = mine + rs_recv[j]
    total = mine[:, :count]
    old_norm = total_over_lanes(mine[:, count:])
    halo_send[...] = total[:, count - bw :]
    after = lax.rem(tm + 1, ntm)
    before = lax.rem(tm + ntm - 1, ntm)
    halo = remote(halo_send, halo_recv, halo_s, halo_r, (after, coef))
    start(halo)

    def forth(window, b):
        hi, lo = split(window)
        return dot_nt(hi, band_hi[b]) + dot_nt(lo, band_hi[b]) + dot_nt(hi, band_lo[b])

    later = [forth(total[:, (b - 1) * bw : (b + 1) * bw], b) for b in range(1, nblocks)]
    halo.wait_recv()
    edge = jnp.where(tm == 0, jnp.zeros_like(halo_recv[...]), halo_recv[...])
    first = forth(jnp.concatenate([edge, total[:, :bw]], axis=1), 0)
    predicted = jnp.concatenate([first] + later, axis=1)
    e_buf[tm] = lane_fold(predicted * predicted)
    for d in range(1, ntm):
        other = lax.rem(tm + d, ntm)
        start(remote(e_buf.at[tm], e_buf.at[tm], e_s.at[other], e_r.at[tm], (other, coef)))
    pred_out, pred_in = back(predicted)
    carry_send[:, :bw] = res_out
    carry_send[:, bw:] = pred_out
    carry = remote(carry_send, carry_recv, carry_s, carry_r, (before, coef))
    start(carry)
    for d in range(1, ntm):
        other = lax.rem(tm + d, ntm)
        remote(e_buf.at[other], e_buf.at[other], e_s.at[other], e_r.at[other], (other, coef)).wait_recv()
    energy = e_buf[0]
    for t in range(1, ntm):
        energy = energy + e_buf[t]
    step = old_norm / total_over_lanes(energy)
    carry.wait_recv()
    last = tm == ntm - 1
    carried = jnp.where(last, jnp.zeros_like(carry_recv[...]), carry_recv[...])

    def with_carried(inner, extra):
        tail = inner[:, count - bw :] + extra
        if count == bw:
            return tail
        return jnp.concatenate([inner[:, : count - bw], tail], axis=1)

    step_wide = widen(step, count)
    ag_buf[coef] = with_carried(res_in, carried[:, :bw]) - step_wide * with_carried(
        pred_in, carried[:, bw:]
    )
    for j in peers:
        start(remote(ag_buf.at[coef], ag_buf.at[coef], ag_s.at[j], ag_r.at[coef], (tm, j)))
    ag2_buf[coef, :, :count] = my_res - step_wide * predicted
    ag2_buf[coef, :, count : count + LANES] = step
    ag2_buf[coef, :, count + LANES :] = old_norm
    for j in peers:
        remote(ag_buf.at[j], ag_buf.at[j], ag_s.at[j], ag_r.at[j], (tm, j)).wait_recv()
    for j in range(ncoef):
        white[j * rpc : (j + 1) * rpc, :] = ag_buf[j]
    whi = white[...].astype(BF16)
    whi32 = whi.astype(F32)
    wboth = jnp.concatenate([whi32, white[...] - whi32], axis=0).astype(BF16)

    def grad_chunk(i):
        a = dot_nn(wboth, dhi[i])
        return a[:right_sides] + a[right_sides:] + dot_nn(whi, dlo[i])

    def to_chips(k):
        remote(psend.at[k], precv.at[k], pair_s.at[k], pair_r.at[k], (partner, coef)).wait_recv()
        xbuf[chip, k] = xbuf[chip, k] + precv[k]
        for q in range(1, nchip):
            other = lax.rem(chip + q, nchip)
            start(
                remote(
                    xbuf.at[chip, k], xbuf.at[chip, k], x_s.at[other, k], x_r.at[chip, k],
                    (other * 2 + core, coef),
                )
            )

    for k in range(half):
        psend[k] = grad_chunk((1 - core) * half + k)
        start(remote(psend.at[k], precv.at[k], pair_s.at[k], pair_r.at[k], (partner, coef)))
        xbuf[chip, k] = grad_chunk(core * half + k)
        to_chips(k)
        if k == 0:
            for j in peers:
                start(
                    remote(ag2_buf.at[coef], ag2_buf.at[coef], ag2_s.at[j], ag2_r.at[coef], (tm, j))
                )

    for j in peers:
        remote(ag2_buf.at[j], ag2_buf.at[j], ag2_s.at[j], ag2_r.at[j], (tm, j)).wait_recv()
    tails = []
    for j in range(ncoef):
        nres[j * rpc : (j + 1) * rpc, :] = ag2_buf[j][:, :count]
        tails.append(ag2_buf[j][:, count:])
    tail = jnp.concatenate(tails, axis=0)
    step_all = widen(tail[:, :LANES], width)
    old_all = tail[:, LANES:]
    sol_copy.wait()
    for i in range(nch):
        at = slice(i * width, (i + 1) * width)
        nsol[:, at] = sv[:, at] + step_all * dv[i]

    squares = jnp.zeros((right_sides, LANES), F32)
    for k in range(half):
        for q in range(1, nchip):
            other = lax.rem(chip + q, nchip)
            remote(
                xbuf.at[other, k], xbuf.at[other, k], x_s.at[other, k], x_r.at[other, k],
                (other * 2 + core, coef),
            ).wait_recv()
        g = xbuf[0, k]
        for t in range(1, nchip):
            g = g + xbuf[t, k]
        at = core * half + k
        gbuf[at] = g
        start(remote(gbuf.at[at], gbuf.at[at], fin_s.at[k], fin_r.at[k], (partner, coef)))
        squares = squares + lane_fold(g * g)

    slot = coef * 2 + core
    row = jnp.sum(squares.T, axis=0, keepdims=True)
    n_buf[slot] = jnp.concatenate([row, jnp.zeros((1, LANES - right_sides), F32)], axis=1)
    others = [(tm, j, j * 2 + core) for j in peers]
    others += [(partner, j, j * 2 + (1 - core)) for j in [coef] + peers]
    for t, j, s in others:
        start(remote(n_buf.at[slot], n_buf.at[slot], n_s.at[s], n_r.at[slot], (t, j)))
    for k in range(half):
        at = (1 - core) * half + k
        remote(gbuf.at[at], gbuf.at[at], fin_s.at[k], fin_r.at[k], (partner, coef)).wait_recv()
    for t, j, s in others:
        remote(n_buf.at[s], n_buf.at[s], n_s.at[s], n_r.at[s], (t, j)).wait_recv()
    row = n_buf[0]
    for s in range(1, 2 * ncoef):
        row = row + n_buf[s]
    new_all = jnp.broadcast_to(row, (LANES, LANES)).T[:right_sides]
    ratio = widen(new_all / old_all, width)
    for i in range(nch):
        ndir[:, i * width : (i + 1) * width] = gbuf[i] + ratio * dv[i]
    for copy in sends:
        copy.wait_send()


def per_device(ntm, ncoef, design, whitening, solution, direction, gradient_prev, residual):
    count, columns = design.shape
    bw = whitening.shape[1]
    rs = direction.shape[1]
    rpc = rs // ncoef
    width = chunk_width(columns)
    nch = columns // width
    half = nch // 2
    nchip = ntm // 2
    nblocks = count // bw
    V = pltpu.VMEM
    D = pltpu.SemaphoreType.DMA
    any_spec = pl.BlockSpec(memory_space=pl.ANY)
    scratch = [
        V((nch, count, width), F32),
        V((nch, count, width), BF16),
        V((nch, count, width), BF16),
        V((nch, rs, width), F32),
        V((rs, columns), F32),
        V((rs, columns), F32),
        V((rs, count), F32),
        V((count, bw), F32),
        V((count, 2 * rs), F32),
        V((nblocks, bw, 2 * bw), BF16),
        V((nblocks, bw, 2 * bw), BF16),
        V((ncoef, rpc, count + LANES), F32),
        V((ncoef, rpc, count + LANES), F32),
        V((rpc, bw), F32),
        V((rpc, bw), F32),
        V((ntm, rpc, LANES), F32),
        V((rpc, 2 * bw), F32),
        V((rpc, 2 * bw), F32),
        V((ncoef, rpc, count), F32),
        V((ncoef, rpc, count + 2 * LANES), F32),
        V((rs, count), F32),
        V((half, rs, width), F32),
        V((half, rs, width), F32),
        V((nchip, half, rs, width), F32),
        V((nch, rs, width), F32),
        V((2 * ncoef, 1, LANES), F32),
        D((nch,)), D((nch,)), D((4,)),
        D((ncoef,)), D((ncoef,)), D, D, D((ntm,)), D((ntm,)), D, D,
        D((ncoef,)), D((ncoef,)), D((ncoef,)), D((ncoef,)),
        D((half,)), D((half,)), D((nchip, half)), D((nchip, half)),
        D((half,)), D((half,)), D((2 * ncoef,)), D((2 * ncoef,)),
    ]
    outs = pl.pallas_call(
        functools.partial(kernel, ntm, ncoef),
        out_shape=(
            jax.ShapeDtypeStruct((rs, columns), F32),
            jax.ShapeDtypeStruct((rs, count), F32),
            jax.ShapeDtypeStruct((rs, columns), F32),
        ),
        in_specs=[any_spec] * 6,
        out_specs=(pl.BlockSpec(memory_space=pltpu.VMEM),) * 3,
        scratch_shapes=scratch,
        compiler_params=pltpu.CompilerParams(
            collective_id=0, has_side_effects=True, vmem_limit_bytes=51 * 2**20
        ),
        cost_estimate=pl.CostEstimate(
            flops=12 * count * columns * rs,
            bytes_accessed=4 * (count * columns + 5 * rs * columns),
            transcendentals=0,
        ),
    )(design, whitening, solution.T, direction.T, gradient_prev.T, residual.T)
    return tuple(o.T for o in outs)


def solution(mesh):
    ntm, ncoef = mesh.shape["tm"], mesh.shape["coef"]
    return jax.shard_map(
        functools.partial(per_device, ntm, ncoef),
        mesh=mesh,
        in_specs=(
            P("tm", "coef"),
            P("tm", None),
            P("coef", None),
            P("coef", None),
            P("coef", None),
            P("tm", None),
        ),
        out_specs=(P("coef", None), P("tm", None), P("coef", None)),
        check_vma=False,
    )
```
